32 devices in a mesh: mp: 4 (over z), store: 4 (over x, core), group: 2 (over y).
Axes of the slice: x: 2, y: 2, z: 4, core: 2. Of those that a mesh axis runs over, the one named last changes fastest.
Arguments:
- gate_pre: bfloat16 [8, 1024, 14336], P(('store', 'group'), None, 'mp'), may hold values from -6 to 6
- up_pre: bfloat16 [8, 1024, 14336], P(('store', 'group'), None, 'mp'), may hold values from -6 to 6
- out_grad: bfloat16 [8, 1024, 8192], P(('store', 'group'), 'mp'), may hold values from -6 to 6
- normed_in: bfloat16 [8, 1024, 8192], P(('store', 'group'), 'mp'), may hold values from -6 to 6
- lengths: int32 [8, 16], P(('store', 'group')), may hold values from 1 to 128, 1024 in all within a row
- w_down: bfloat16 [14336, 8192], P('mp'), may hold values from -0.046875 to 0.046875
- proj_hidden: bfloat16 [14336, 64], P('mp'), may hold values from -0.046875 to 0.046875
- proj_gate: bfloat16 [14336, 64], P('mp'), may hold values from -0.046875 to 0.046875
- proj_up: bfloat16 [14336, 64], P('mp'), may hold values from -0.046875 to 0.046875
- proj_outgrad: bfloat16 [8192, 64], replicated, may hold values from -0.0625 to 0.0625
- proj_input: bfloat16 [8192, 64], replicated, may hold values from -0.0625 to 0.0625
- datastore: bfloat16 [16384, 12288], P(('store', 'group'), 'mp'), may hold values from -0.011962891 to 0.011962891
Outputs:
- scores: float32 [128, 16384], P('mp', ('store', 'group'))
The draws below stay inside these ranges and needn't reach their ends.
Inputs may be any that keep to these rules, and one draw needn't show every extreme that they name: Each row holds 16 lengths of 1 or more summing to 1024; the longest of each row is exactly 128.
All inputs are finite; a program needn't handle non-finite values.
Results may differ from the reference program's by a relative error of at most 0.0041.
Values may be sent and summed in bfloat16 or wider, within the bound.
A program may use at most 192 MiB of HBM per device.

```python
import math
import jax
import jax.numpy as jnp
import numpy as np
from jax import lax

D = 8192
FF = 14336
R = 64
TOK = 1024
EX = 16
LMAX = 128
FEAT = 12288
REPLICAS = 8
QUERIES = 128
ROWS = 16384


def block_scale(key, shape, pieces, smallest, top_value):
    level, own = 1.0, jax.random.fold_in(key, 6)
    for dim, blocks in pieces:
        steps = jnp.exp(jax.random.uniform(jax.random.fold_in(own, dim), (blocks,), jnp.float32, smallest / len(pieces), top_value / len(pieces)))
        level = level * jnp.repeat(steps, shape[dim] // blocks).reshape([-1 if axis == dim else 1 for axis in range(len(shape))])
    return level


def profile(number_of, total, most, lean):
    weights = [(1 << 20) // math.isqrt(grade ** lean) + 1 for grade in range(2, number_of + 1)]
    surplus, counts = total - most - (number_of - 1), [1] * (number_of - 1)
    while surplus > 0:
        candidates = [i for i in range(number_of - 1) if counts[i] < most]
        whole, remaining = sum([weights[i] for i in candidates]), surplus
        for i in candidates:
            more = min(most - counts[i], max(1, remaining * weights[i] // whole), surplus)
            counts[i] = counts[i] + more
            surplus = surplus - more
    return np.array([most] + counts)


def uneven_parts(rng, number_of, total, most, lean):
    if number_of == 2:
        one = jax.random.randint(rng, (), max(1, total - most), min(most, total - 1) + 1)
        return jnp.stack([one, total - one])
    sizes = jnp.asarray(profile(number_of, total, most, lean), jnp.int32)
    twos = (number_of - 1) // 2
    donor, sink = sizes[1:1 + 2 * twos:2], sizes[2:2 + 2 * twos:2]
    margin = jnp.minimum(donor - 1, most - sink)
    shifted = jax.random.randint(jax.random.fold_in(rng, 1), (twos,), 0, 1 << 20) % (margin + 1)
    sizes = sizes.at[1:1 + 2 * twos:2].set(donor - shifted).at[2:2 + 2 * twos:2].set(sink + shifted)
    return sizes[jax.random.permutation(jax.random.fold_in(rng, 2), number_of)]


def scatter_about(stream_key, shape, deviation, most, split=(), kind=jnp.bfloat16):
    result = jax.random.normal(stream_key, shape, jnp.float32) * deviation
    if len(split) > 0:
        result = block_scale(stream_key, shape, split, -0.22, 0.18) * result
    return jnp.clip(result, min=-most, max=most).astype(kind)


def setup_inputs(seed: int = 0) -> dict:
    arg_keys = jax.random.split(jax.random.key(seed), 13)
    return {
        "gate_pre": scatter_about(arg_keys[0], (REPLICAS, TOK, FF), 1.0, 6.0, ((0, 8), (2, 4))),
        "up_pre": scatter_about(arg_keys[1], (REPLICAS, TOK, FF), 1.0, 6.0, ((0, 8), (2, 4))),
        "out_grad": scatter_about(arg_keys[2], (REPLICAS, TOK, D), 1.0, 6.0, ((0, 8), (1, 4))),
        "normed_in": scatter_about(arg_keys[3], (REPLICAS, TOK, D), 1.0, 6.0, ((0, 8), (1, 4))),
        "lengths": jax.vmap(lambda own: uneven_parts(own, EX, TOK, LMAX, 2))(jax.random.split(arg_keys[4], REPLICAS)).reshape((REPLICAS, EX)).astype(jnp.int32),
        "w_down": scatter_about(arg_keys[5], (FF, D), FF ** -0.5, 0.046875, ((0, 4),)),
        "proj_hidden": scatter_about(arg_keys[6], (FF, R), FF ** -0.5, 0.046875, ((0, 4),)),
        "proj_gate": scatter_about(arg_keys[7], (FF, R), FF ** -0.5, 0.046875, ((0, 4),)),
        "proj_up": scatter_about(arg_keys[8], (FF, R), FF ** -0.5, 0.046875, ((0, 4),)),
        "proj_outgrad": scatter_about(arg_keys[9], (D, R), D ** -0.5, 0.0625),
        "proj_input": scatter_about(arg_keys[10], (D, R), D ** -0.5, 0.0625),
        "datastore": scatter_about(arg_keys[11], (ROWS, FEAT), 0.002, 0.011962891, ((0, 8), (1, 4))),
    }


def outer_sums(member, left, right):
    weighted = (member[:, :, None] * left[:, None, :]).reshape(left.shape[0], -1)
    summed = lax.dot_general(weighted, right, (((0,), (0,)), ((), ())), precision=lax.Precision.HIGHEST, preferred_element_type=jnp.float32)
    return summed.reshape(member.shape[1], -1)


def reference(gate_pre, up_pre, out_grad, normed_in, lengths, w_down, proj_hidden, proj_gate, proj_up, proj_outgrad, proj_input, datastore):
    def one_replica(items):
        gate_raw, up_raw, grad_rows, input_rows, example_lengths = items
        gate_val = gate_raw.astype(jnp.float32)
        up_val = up_raw.astype(jnp.float32)
        gate_sig = jax.nn.sigmoid(gate_val)
        silu_gate = gate_val * gate_sig
        hidden = (silu_gate * up_val).astype(jnp.bfloat16)
        hidden_grad = jnp.dot(grad_rows, w_down.T, preferred_element_type=jnp.float32)
        gate_grad = (hidden_grad * up_val * gate_sig * (1.0 + gate_val * (1.0 - gate_sig))).astype(jnp.bfloat16)
        up_grad = (hidden_grad * silu_gate).astype(jnp.bfloat16)
        down_in = jnp.dot(hidden, proj_hidden, preferred_element_type=jnp.float32)
        gate_out = jnp.dot(gate_grad, proj_gate, preferred_element_type=jnp.float32)
        up_out = jnp.dot(up_grad, proj_up, preferred_element_type=jnp.float32)
        down_out = jnp.dot(grad_rows, proj_outgrad, preferred_element_type=jnp.float32)
        gate_in = jnp.dot(input_rows, proj_input, preferred_element_type=jnp.float32)
        seq_ends = jnp.cumsum(example_lengths).astype(jnp.int32)
        seq_starts = seq_ends - example_lengths
        positions = jnp.arange(TOK, dtype=jnp.int32)
        member = ((positions[:, None] >= seq_starts[None, :]) & (positions[:, None] < seq_ends[None, :])).astype(jnp.float32)
        feats = jnp.concatenate([outer_sums(member, down_in, down_out), outer_sums(member, gate_in, gate_out), outer_sums(member, gate_in, up_out)], axis=1)
        return feats.astype(jnp.bfloat16)

    feats = lax.map(one_replica, (gate_pre, up_pre, out_grad, normed_in, lengths))
    query_feats = feats.reshape(QUERIES, FEAT)
    return jnp.dot(query_feats, datastore.T, preferred_element_type=jnp.float32)
```

```python
import jax
import jax.numpy as jnp
from jax import lax
from jax.sharding import PartitionSpec as P


def membership(seq_starts, seq_ends, count):
    positions = jnp.arange(count, dtype=jnp.int32)
    return (
        (positions[:, None] >= seq_starts[None, :]) & (positions[:, None] < seq_ends[None, :])
    ).astype(jnp.float32)


def outer_sums(member, left, right):
    weighted = (member[:, :, None] * left[:, None, :]).reshape(left.shape[0], -1)
    summed = lax.dot_general(
        weighted,
        right,
        (((0,), (0,)), ((), ())),
        precision=lax.Precision.HIGHEST,
        preferred_element_type=jnp.float32,
    )
    return summed.reshape(member.shape[1], -1)


def on_device(
    gate_pre,
    up_pre,
    out_grad,
    normed_in,
    lengths,
    w_down,
    proj_hidden,
    proj_gate,
    proj_up,
    proj_outgrad,
    proj_input,
    datastore,
):
    gate_val = gate_pre[0].astype(jnp.float32)
    up_val = up_pre[0].astype(jnp.float32)
    gate_sig = jax.nn.sigmoid(gate_val)
    silu_gate = gate_val * gate_sig
    hidden = (silu_gate * up_val).astype(jnp.bfloat16)
    grad_own = out_grad[0]
    input_own = normed_in[0]
    hidden_grad = lax.dot_general(
        lax.all_gather(grad_own, "mp", axis=0, tiled=True),
        w_down,
        (((1,), (1,)), ((), ())),
        preferred_element_type=jnp.float32,
    )
    gate_grad = (hidden_grad * up_val * gate_sig * (1.0 + gate_val * (1.0 - gate_sig))).astype(
        jnp.bfloat16
    )
    up_grad = (hidden_grad * silu_gate).astype(jnp.bfloat16)
    down_in_part = jnp.dot(hidden, proj_hidden, preferred_element_type=jnp.float32)
    gate_out_part = jnp.dot(gate_grad, proj_gate, preferred_element_type=jnp.float32)
    up_out_part = jnp.dot(up_grad, proj_up, preferred_element_type=jnp.float32)
    down_out_own = jnp.dot(grad_own, proj_outgrad, preferred_element_type=jnp.float32)
    gate_in_own = jnp.dot(input_own, proj_input, preferred_element_type=jnp.float32)
    example_lengths = lengths[0]
    order = jnp.arange(example_lengths.shape[0], dtype=jnp.int32)
    seq_ends = jnp.sum(
        jnp.where(order[None, :] <= order[:, None], example_lengths[None, :], 0), axis=1
    )
    seq_starts = seq_ends - example_lengths
    all_count = gate_val.shape[0]
    gate_in, down_out = (
        lax.all_gather(gate_in_own, "mp", axis=0, tiled=True),
        lax.all_gather(down_out_own, "mp", axis=0, tiled=True),
    )
    member = membership(seq_starts, seq_ends, all_count)
    partial_value = jnp.concatenate(
        [
            outer_sums(member, down_in_part, down_out),
            outer_sums(member, gate_in, gate_out_part),
            outer_sums(member, gate_in, up_out_part),
        ],
        axis=1,
    )
    feats = lax.psum_scatter(partial_value, "mp", scatter_dimension=1, tiled=True).astype(
        jnp.bfloat16
    )
    queries = lax.all_gather(feats, ("store", "group"), axis=0, tiled=True)
    partial_scores = lax.dot_general(
        queries, datastore, (((1,), (1,)), ((), ())), preferred_element_type=jnp.float32
    )
    return lax.psum_scatter(partial_scores, "mp", scatter_dimension=0, tiled=True)


def solution(mesh):
    return jax.shard_map(
        on_device,
        mesh=mesh,
        in_specs=(
            P(("store", "group"), None, "mp"),
            P(("store", "group"), None, "mp"),
            P(("store", "group"), "mp", None),
            P(("store", "group"), "mp", None),
            P(("store", "group"), None),
            P("mp", None),
            P("mp", None),
            P("mp", None),
            P("mp", None),
            P(),
            P(),
            P(("store", "group"), "mp"),
        ),
        out_specs=P("mp", ("store", "group")),
        check_vma=False,
    )
```

```python
import functools

import jax
import jax.numpy as jnp
from jax import lax
from jax.experimental import pallas as pl
from jax.experimental.pallas import tpu as pltpu
from jax.sharding import PartitionSpec as P

MESH = pl.DeviceIdType.MESH
NT = (((1,), (1,)), ((), ()))
VMEM_LIMIT = 56 * 2**20


def tile_of(size, most):
    return max(t for t in range(128, most + 1, 128) if size % t == 0)


def gather_kernel(
    n, chunks, tile,
    og, w, gate, up, ph, pg, pu, po, ni, pi,
    down_in, gate_out, up_out, down_out, gate_in,
    held, acc, gin, send_sem, recv_sem, local_sem, gin_send, gin_recv,
):
    d = lax.axis_index("mp")
    tokens, width = og.shape
    depth = width // chunks
    tiles = w.shape[0] // tile
    left, right = lax.rem(d + n - 1, n), lax.rem(d + 1, n)

    barrier = pltpu.get_barrier_semaphore()
    for k in range(1, n):
        pl.semaphore_signal(
            barrier, inc=1, device_id={"mp": lax.rem(d + k, n)}, device_id_type=MESH
        )
    pl.semaphore_wait(barrier, n - 1)

    def columns(c):
        return pl.ds(pl.multiple_of(c * depth, depth), depth)

    def rows(p):
        return pl.ds(pl.multiple_of(p * tokens, tokens), tokens)

    def local(c):
        return pltpu.make_async_copy(og.at[:, columns(c)], held.at[d, c], local_sem.at[c])

    def remote(way, p, c, own):
        return pltpu.make_async_remote_copy(
            src_ref=og.at[:, columns(c)] if own else held.at[p, c],
            dst_ref=held.at[p, c],
            send_sem=send_sem.at[way, p, c],
            recv_sem=recv_sem.at[p, c],
            device_id={"mp": left if way == 0 else right},
            device_id_type=MESH,
        )

    has_left, has_right = d > 0, d < n - 1

    def send_own(c, carry):
        @pl.when(has_left)
        def _():
            remote(0, d, c, True).start()

        @pl.when(has_right)
        def _():
            remote(1, d, c, True).start()

        local(c).start()
        return carry

    lax.fori_loop(0, chunks, send_own, 0)

    for ref in (down_in, gate_out, up_out, down_out):
        ref[...] = jnp.zeros_like(ref)

    def own_gate_in(ni_ref, pi_ref):
        part = jnp.dot(ni_ref[...], pi_ref[...], preferred_element_type=jnp.float32)
        first = pl.program_id(0) == 0

        @pl.when(first)
        def _():
            gin[d] = part

        @pl.when(jnp.logical_not(first))
        def _():
            gin[d] += part

    pltpu.emit_pipeline(
        own_gate_in,
        grid=(chunks,),
        in_specs=[
            pl.BlockSpec((tokens, depth), lambda c: (0, c)),
            pl.BlockSpec((depth, pi.shape[1]), lambda c: (c, 0)),
        ],
    )(ni, pi)

    def gin_copy(k):
        return pltpu.make_async_remote_copy(
            src_ref=gin.at[d],
            dst_ref=gin.at[d],
            send_sem=gin_send.at[k],
            recv_sem=gin_recv.at[k],
            device_id={"mp": lax.rem(d + k, n)},
            device_id_type=MESH,
        )

    for k in range(1, n):
        gin_copy(k).start()

    def wait_local(c, carry):
        local(c).wait()
        return carry

    lax.fori_loop(0, chunks, wait_local, 0)

    def step(s, carry):
        shards = (d + s, d - s)
        valid = (shards[0] < n, (s > 0) & (shards[1] >= 0))
        at = (jnp.minimum(shards[0], n - 1), jnp.maximum(shards[1], 0))
        onward = (has_left, has_right)

        def arrive(c):
            for way in range(2):
                @pl.when(valid[way] & (s > 0))
                def _():
                    remote(way, at[way], c, False).wait_recv()

                    @pl.when(onward[way])
                    def _():
                        remote(way, at[way], c, False).start()

            for way in range(2):
                @pl.when(valid[way])
                def _():
                    down_out[rows(at[way]), :] += jnp.dot(
                        held[at[way], c],
                        po[columns(c), :],
                        preferred_element_type=jnp.float32,
                    )

        def chunk(c, inner):
            arrive(c)

            def body(w_ref):
                j = pl.program_id(0)
                for way in range(2):
                    @pl.when(valid[way])
                    def _():
                        part = lax.dot_general(
                            held[at[way], c], w_ref[...], NT,
                            preferred_element_type=jnp.float32,
                        )

                        @pl.when(c == 0)
                        def _():
                            acc[way, j] = part

                        @pl.when(c > 0)
                        def _():
                            acc[way, j] += part

            pltpu.emit_pipeline(
                body,
                grid=(tiles,),
                in_specs=[pl.BlockSpec((tile, depth), lambda j: (j, c))],
            )(w)
            return inner

        lax.fori_loop(0, chunks - 1, chunk, 0)
        last = chunks - 1
        arrive(last)

        def finish(w_ref, g0, u0, g1, u1, ph_ref, pg_ref, pu_ref):
            j = pl.program_id(0)
            for way, g_ref, u_ref in ((0, g0, u0), (1, g1, u1)):
                @pl.when(valid[way])
                def _():
                    grad = acc[way, j] + lax.dot_general(
                        held[at[way], last], w_ref[...], NT,
                        preferred_element_type=jnp.float32,
                    )
                    g = g_ref[...].astype(jnp.float32)
                    u = u_ref[...].astype(jnp.float32)
                    sig = jax.nn.sigmoid(g)
                    silu = g * sig
                    hidden = (silu * u).astype(jnp.bfloat16)
                    gate_grad = (grad * u * sig * (1.0 + g * (1.0 - sig))).astype(jnp.bfloat16)
                    up_grad = (grad * silu).astype(jnp.bfloat16)
                    at_rows = rows(at[way])
                    for out, value, proj in (
                        (down_in, hidden, ph_ref),
                        (gate_out, gate_grad, pg_ref),
                        (up_out, up_grad, pu_ref),
                    ):
                        out[at_rows, :] += jnp.dot(
                            value, proj[...], preferred_element_type=jnp.float32
                        )

        elem = lambda way: pl.BlockSpec((tokens, tile), lambda j: (at[way], j))
        proj = pl.BlockSpec((tile, ph.shape[1]), lambda j: (j, 0))
        pltpu.emit_pipeline(
            finish,
            grid=(tiles,),
            in_specs=[
                pl.BlockSpec((tile, depth), lambda j: (j, last)),
                elem(0), elem(0), elem(1), elem(1), proj, proj, proj,
            ],
        )(w, gate, up, gate, up, ph, pg, pu)
        return carry

    lax.fori_loop(0, n, step, 0)

    for k in range(1, n):
        gin_copy(k).wait()
    for p in range(n):
        gate_in[p * tokens:(p + 1) * tokens, :] = gin[p]

    def drain(p, carry):
        def one(c, inner):
            @pl.when(has_left & (p >= d))
            def _():
                remote(0, p, c, False).wait_send()

            @pl.when(has_right & (p <= d))
            def _():
                remote(1, p, c, False).wait_send()

            return inner

        return lax.fori_loop(0, chunks, one, carry)

    lax.fori_loop(0, n, drain, 0)


def gathered(n, og, w, gate, up, ph, pg, pu, po, ni, pi):
    tokens, width = og.shape
    units, r = ph.shape
    chunks = 4
    depth = width // chunks
    tile = tile_of(units, 512)
    out = jax.ShapeDtypeStruct((n * tokens, r), jnp.float32)
    hbm = pl.BlockSpec(memory_space=pl.ANY)
    vmem = pl.BlockSpec(memory_space=pltpu.VMEM)
    return pl.pallas_call(
        functools.partial(gather_kernel, n, chunks, tile),
        out_shape=[out] * 5,
        in_specs=[hbm] * 7 + [vmem, hbm, hbm],
        out_specs=[vmem] * 5,
        scratch_shapes=[
            pltpu.VMEM((n, chunks, tokens, depth), jnp.bfloat16),
            pltpu.VMEM((2, units // tile, tokens, tile), jnp.float32),
            pltpu.VMEM((n, tokens, r), jnp.float32),
            pltpu.SemaphoreType.DMA((2, n, chunks)),
            pltpu.SemaphoreType.DMA((n, chunks)),
            pltpu.SemaphoreType.DMA((chunks,)),
            pltpu.SemaphoreType.DMA((n,)),
            pltpu.SemaphoreType.DMA((n,)),
        ],
        compiler_params=pltpu.CompilerParams(
            collective_id=0, has_side_effects=True, vmem_limit_bytes=VMEM_LIMIT
        ),
        name="gather_grads",
    )(og, w, gate, up, ph, pg, pu, po, ni, pi)


def score_kernel(
    n, stores, groups, tile,
    parts, store_rows, out,
    feats_in, queries, store_buf, sent, own, back_in,
    store_sem, fs, fr, qs, qr, bs, br,
):
    d = lax.axis_index("mp")
    sx, gx = lax.axis_index("store"), lax.axis_index("group")
    me = sx * groups + gx
    replicas = stores * groups
    examples = parts.shape[1]
    block = own.shape[0]

    load = pltpu.make_async_copy(store_rows, store_buf, store_sem)
    load.start()

    def peer(k):
        return {"mp": lax.rem(d + k, n)}

    def mate(k):
        other = lax.rem(me + k, replicas)
        return {"store": other // groups, "group": lax.rem(other, groups)}

    barrier = pltpu.get_barrier_semaphore()
    for k in range(1, n):
        pl.semaphore_signal(barrier, inc=1, device_id=peer(k), device_id_type=MESH)
    for k in range(1, replicas):
        pl.semaphore_signal(barrier, inc=1, device_id=mate(k), device_id_type=MESH)
    pl.semaphore_wait(barrier, n + replicas - 2)

    def feats_copy(k):
        return pltpu.make_async_remote_copy(
            src_ref=parts.at[lax.rem(d + k, n)], dst_ref=feats_in.at[k - 1],
            send_sem=fs.at[k - 1], recv_sem=fr.at[k - 1],
            device_id=peer(k), device_id_type=MESH,
        )

    for k in range(1, n):
        feats_copy(k).start()
    total = parts[d].astype(jnp.float32)
    for k in range(1, n):
        feats_copy(k).wait_recv()
        total += feats_in[k - 1].astype(jnp.float32)
    my_rows = pl.ds(pl.multiple_of(me * examples, examples), examples)
    queries[my_rows, :] = total.astype(jnp.bfloat16)

    def query_copy(k):
        return pltpu.make_async_remote_copy(
            src_ref=queries.at[my_rows, :], dst_ref=queries.at[my_rows, :],
            send_sem=qs.at[k - 1], recv_sem=qr.at[k - 1],
            device_id=mate(k), device_id_type=MESH,
        )

    for k in range(1, replicas):
        query_copy(k).start()
    load.wait()
    for k in range(1, replicas):
        query_copy(k).wait_recv()

    def scores(j, carry):
        cols = pl.ds(pl.multiple_of(j * tile, tile), tile)
        part = lax.dot_general(
            queries[...], store_buf[cols, :], NT, preferred_element_type=jnp.float32
        )
        for p in range(n):
            piece = part[p * block:(p + 1) * block, :]
            sent[p, :, cols] = piece.astype(sent.dtype)

            @pl.when(p == d)
            def _():
                own[:, cols] = piece

        return carry

    lax.fori_loop(0, store_buf.shape[0] // tile, scores, 0)

    def back_copy(k):
        return pltpu.make_async_remote_copy(
            src_ref=sent.at[lax.rem(d + k, n)], dst_ref=back_in.at[k - 1],
            send_sem=bs.at[k - 1], recv_sem=br.at[k - 1],
            device_id=peer(k), device_id_type=MESH,
        )

    for k in range(1, n):
        back_copy(k).start()
    for k in range(1, n):
        back_copy(k).wait_recv()
        own[...] += back_in[k - 1].astype(jnp.float32)
    out[...] = own[...]
    for k in range(1, n):
        feats_copy(k).wait_send()
        back_copy(k).wait_send()
    for k in range(1, replicas):
        query_copy(k).wait_send()


def scored(n, stores, groups, parts, datastore):
    _, examples, width = parts.shape
    count = datastore.shape[0]
    replicas = stores * groups
    block = replicas * examples // n
    sent = jnp.bfloat16 if block % 16 == 0 else jnp.float32
    vmem = pl.BlockSpec(memory_space=pltpu.VMEM)
    dma = pltpu.SemaphoreType.DMA
    return pl.pallas_call(
        functools.partial(score_kernel, n, stores, groups, tile_of(count, 512)),
        out_shape=jax.ShapeDtypeStruct((block, count), jnp.float32),
        in_specs=[vmem, pl.BlockSpec(memory_space=pl.ANY)],
        out_specs=vmem,
        scratch_shapes=[
            pltpu.VMEM((n - 1, examples, width), jnp.bfloat16),
            pltpu.VMEM((replicas * examples, width), jnp.bfloat16),
            pltpu.VMEM(datastore.shape, jnp.bfloat16),
            pltpu.VMEM((n, block, count), sent),
            pltpu.VMEM((block, count), jnp.float32),
            pltpu.VMEM((n - 1, block, count), sent),
            dma(()), dma((n - 1,)), dma((n - 1,)),
            dma((replicas - 1,)), dma((replicas - 1,)),
            dma((n - 1,)), dma((n - 1,)),
        ],
        compiler_params=pltpu.CompilerParams(
            collective_id=1, has_side_effects=True, vmem_limit_bytes=VMEM_LIMIT
        ),
        name="exchange_scores",
    )(parts, datastore)


def outer_sums(member, left, right):
    weighted = (member[:, :, None] * left[:, None, :]).reshape(left.shape[0], -1)
    summed = lax.dot_general(
        weighted,
        right,
        (((0,), (0,)), ((), ())),
        precision=lax.Precision.HIGHEST,
        preferred_element_type=jnp.float32,
    )
    return summed.reshape(member.shape[1], left.shape[1], right.shape[1])


def on_device(
    n, stores, groups,
    gate_pre, up_pre, out_grad, normed_in, lengths, w_down,
    proj_hidden, proj_gate, proj_up, proj_outgrad, proj_input, datastore,
):
    count = gate_pre.shape[1]
    r = proj_hidden.shape[1]
    example_lengths = lengths[0]
    examples = example_lengths.shape[0]
    order = jnp.arange(examples, dtype=jnp.int32)
    ends = jnp.sum(
        jnp.where(order[None, :] <= order[:, None], example_lengths[None, :], 0), axis=1
    )
    starts = ends - example_lengths
    positions = jnp.arange(count, dtype=jnp.int32)
    member = (
        (positions[:, None] >= starts[None, :]) & (positions[:, None] < ends[None, :])
    ).astype(jnp.float32)

    down_in, gate_out, up_out, down_out, gate_in = gathered(
        n, out_grad[0], w_down, gate_pre[0], up_pre[0],
        proj_hidden, proj_gate, proj_up, proj_outgrad, normed_in[0], proj_input,
    )
    down = outer_sums(member, down_in, down_out)
    both = outer_sums(member, gate_in, jnp.concatenate([gate_out, up_out], axis=1))
    feats = jnp.concatenate([down, both[:, :, :r], both[:, :, r:]], axis=1)
    parts = (
        feats.astype(jnp.bfloat16)
        .reshape(examples, n, -1)
        .transpose(1, 0, 2)
    )
    return scored(n, stores, groups, parts, datastore)


def solution(mesh):
    sizes = mesh.shape
    return jax.shard_map(
        functools.partial(on_device, sizes["mp"], sizes["store"], sizes["group"]),
        mesh=mesh,
        in_specs=(
            P(("store", "group"), None, "mp"),
            P(("store", "group"), None, "mp"),
            P(("store", "group"), "mp", None),
            P(("store", "group"), "mp", None),
            P(("store", "group"), None),
            P("mp", None),
            P("mp", None),
            P("mp", None),
            P("mp", None),
            P(),
            P(),
            P(("store", "group"), "mp"),
        ),
        out_specs=P("mp", ("store", "group")),
        check_vma=False,
    )
```

```python
import functools

import jax
import jax.numpy as jnp
from jax import lax
from jax.experimental import pallas as pl
from jax.experimental.pallas import tpu as pltpu
from jax.sharding import PartitionSpec as P

MESH = pl.DeviceIdType.MESH
NT = (((1,), (1,)), ((), ()))
VMEM_LIMIT = 56 * 2**20
CHUNKS = 4


def tile_of(size, most):
    return max(t for t in range(128, most + 1, 128) if size % t == 0)


def gather_kernel(
    n, chunks, tile,
    og, w, gate, up, ph, pg, pu, po, ni, pi, member,
    down_sums, both_sums,
    down_in, gate_out, up_out, down_out, held, acc, gin, send_sem, recv_sem, local_sem, gin_send, gin_recv,
):
    d = lax.axis_index("mp")
    tokens, width = og.shape
    depth = width // chunks
    tiles = w.shape[0] // tile
    left, right = lax.rem(d + n - 1, n), lax.rem(d + 1, n)

    barrier = pltpu.get_barrier_semaphore()
    for k in range(1, n):
        pl.semaphore_signal(
            barrier, inc=1, device_id={"mp": lax.rem(d + k, n)}, device_id_type=MESH
        )
    pl.semaphore_wait(barrier, n - 1)

    def columns(c):
        return pl.ds(pl.multiple_of(c * depth, depth), depth)

    def rows(p):
        return pl.ds(pl.multiple_of(p * tokens, tokens), tokens)

    def local(c):
        return pltpu.make_async_copy(og.at[:, columns(c)], held.at[d, c], local_sem.at[c])

    def remote(way, p, c, own):
        return pltpu.make_async_remote_copy(
            src_ref=og.at[:, columns(c)] if own else held.at[p, c],
            dst_ref=held.at[p, c],
            send_sem=send_sem.at[way, p, c],
            recv_sem=recv_sem.at[p, c],
            device_id={"mp": left if way == 0 else right},
            device_id_type=MESH,
        )

    has_left, has_right = d > 0, d < n - 1

    def send_own(c, carry):
        @pl.when(has_left)
        def _():
            remote(0, d, c, True).start()

        @pl.when(has_right)
        def _():
            remote(1, d, c, True).start()

        local(c).start()
        return carry

    lax.fori_loop(0, chunks, send_own, 0)

    for ref in (down_in, gate_out, up_out, down_out, down_sums, both_sums):
        ref[...] = jnp.zeros_like(ref)

    def own_gate_in(ni_ref, pi_ref):
        part = lax.dot_general(
            ni_ref[...], pi_ref[...], NT, preferred_element_type=jnp.float32
        )
        first = pl.program_id(0) == 0

        @pl.when(first)
        def _():
            gin[d] = part

        @pl.when(jnp.logical_not(first))
        def _():
            gin[d] += part

    pltpu.emit_pipeline(
        own_gate_in,
        grid=(chunks,),
        in_specs=[
            pl.BlockSpec((tokens, depth), lambda c: (0, c)),
            pl.BlockSpec((pi.shape[0], depth), lambda c: (0, c)),
        ],
    )(ni, pi)

    def gin_copy(k):
        return pltpu.make_async_remote_copy(
            src_ref=gin.at[d],
            dst_ref=gin.at[d],
            send_sem=gin_send.at[k],
            recv_sem=gin_recv.at[k],
            device_id={"mp": lax.rem(d + k, n)},
            device_id_type=MESH,
        )

    for k in range(1, n):
        gin_copy(k).start()

    def wait_local(c, carry):
        local(c).wait()
        return carry

    lax.fori_loop(0, chunks, wait_local, 0)

    def step(s, carry):
        shards = (d + s, d - s)
        valid = (shards[0] < n, (s > 0) & (shards[1] >= 0))
        at = (jnp.minimum(shards[0], n - 1), jnp.maximum(shards[1], 0))
        onward = (has_left, has_right)

        def arrive(c):
            for way in range(2):
                @pl.when(valid[way] & (s > 0))
                def _():
                    remote(way, at[way], c, False).wait_recv()

                    @pl.when(onward[way])
                    def _():
                        remote(way, at[way], c, False).start()

            for way in range(2):
                @pl.when(valid[way])
                def _():
                    down_out[rows(at[way]), :] += lax.dot_general(
                        held[at[way], c],
                        po[:, columns(c)],
                        NT,
                        preferred_element_type=jnp.float32,
                    )

        def chunk(c, inner):
            arrive(c)

            def body(w_ref):
                j = pl.program_id(0)
                for way in range(2):
                    @pl.when(valid[way])
                    def _():
                        part = lax.dot_general(
                            held[at[way], c], w_ref[...], NT,
                            preferred_element_type=jnp.float32,
                        )

                        @pl.when(c == 0)
                        def _():
                            acc[way, j] = part

                        @pl.when(c > 0)
                        def _():
                            acc[way, j] += part

            pltpu.emit_pipeline(
                body,
                grid=(tiles,),
                in_specs=[pl.BlockSpec((tile, depth), lambda j: (j, c))],
            )(w)
            return inner

        lax.fori_loop(0, chunks - 1, chunk, 0)
        last = chunks - 1
        arrive(last)

        def finish(w_ref, g0, u0, g1, u1, ph_ref, pg_ref, pu_ref):
            j = pl.program_id(0)
            for way, g_ref, u_ref in ((0, g0, u0), (1, g1, u1)):
                @pl.when(valid[way])
                def _():
                    grad = acc[way, j] + lax.dot_general(
                        held[at[way], last], w_ref[...], NT,
                        preferred_element_type=jnp.float32,
                    )
                    g = g_ref[...].astype(jnp.float32)
                    u = u_ref[...].astype(jnp.float32)
                    sig = jax.nn.sigmoid(g)
                    silu = g * sig
                    hidden = (silu * u).astype(jnp.bfloat16)
                    gate_grad = (grad * u * sig * (1.0 + g * (1.0 - sig))).astype(jnp.bfloat16)
                    up_grad = (grad * silu).astype(jnp.bfloat16)
                    at_rows = rows(at[way])
                    for out, value, proj in (
                        (down_in, hidden, ph_ref),
                        (gate_out, gate_grad, pg_ref),
                        (up_out, up_grad, pu_ref),
                    ):
                        out[at_rows, :] += lax.dot_general(
                            value, proj[...], NT, preferred_element_type=jnp.float32
                        )

        elem = lambda way: pl.BlockSpec((tokens, tile), lambda j: (at[way], j))
        proj = pl.BlockSpec((ph.shape[0], tile), lambda j: (0, j))
        pltpu.emit_pipeline(
            finish,
            grid=(tiles,),
            in_specs=[
                pl.BlockSpec((tile, depth), lambda j: (j, last)),
                elem(0), elem(0), elem(1), elem(1), proj, proj, proj,
            ],
        )(w, gate, up, gate, up, ph, pg, pu)

        @pl.when(s == 0)
        def _():
            for k in range(1, n):
                gin_copy(k).wait()

        for way in range(2):
            @pl.when(valid[way])
            def _():
                at_rows = rows(at[way])
                of = member[at[way]]

                def add(sums, value, other):
                    flat = value.T
                    weighted = jnp.concatenate(
                        [flat * of[e:e + 1, :] for e in range(of.shape[0])], axis=0
                    )
                    sums[...] += jnp.dot(
                        weighted, other,
                        precision=lax.Precision.HIGHEST,
                        preferred_element_type=jnp.float32,
                    )

                add(down_sums, down_in[at_rows, :], down_out[at_rows, :])
                add(
                    both_sums, gin[at[way]],
                    jnp.concatenate([gate_out[at_rows, :], up_out[at_rows, :]], axis=1),
                )

        return carry

    lax.fori_loop(0, n, step, 0)

    def drain(p, carry):
        def one(c, inner):
            @pl.when(has_left & (p >= d))
            def _():
                remote(0, p, c, False).wait_send()

            @pl.when(has_right & (p <= d))
            def _():
                remote(1, p, c, False).wait_send()

            return inner

        return lax.fori_loop(0, chunks, one, carry)

    lax.fori_loop(0, n, drain, 0)


def gathered(n, og, w, gate, up, ph, pg, pu, po, ni, pi, member):
    tokens, width = og.shape
    r, units = ph.shape
    examples = member.shape[1]
    chunks = CHUNKS
    depth = width // chunks
    tile = tile_of(units, 512)
    hbm = pl.BlockSpec(memory_space=pl.ANY)
    vmem = pl.BlockSpec(memory_space=pltpu.VMEM)
    return pl.pallas_call(
        functools.partial(gather_kernel, n, chunks, tile),
        out_shape=[
            jax.ShapeDtypeStruct((examples * r, r), jnp.float32),
            jax.ShapeDtypeStruct((examples * r, 2 * r), jnp.float32),
        ],
        in_specs=[hbm] * 7 + [vmem, hbm, hbm, vmem],
        out_specs=[vmem] * 2,
        scratch_shapes=[
            *[pltpu.VMEM((n * tokens, r), jnp.float32)] * 4,
            pltpu.VMEM((n, chunks, tokens, depth), jnp.bfloat16),
            pltpu.VMEM((2, units // tile, tokens, tile), jnp.float32),
            pltpu.VMEM((n, tokens, r), jnp.float32),
            pltpu.SemaphoreType.DMA((2, n, chunks)),
            pltpu.SemaphoreType.DMA((n, chunks)),
            pltpu.SemaphoreType.DMA((chunks,)),
            pltpu.SemaphoreType.DMA((n,)),
            pltpu.SemaphoreType.DMA((n,)),
        ],
        compiler_params=pltpu.CompilerParams(
            collective_id=0, has_side_effects=True, vmem_limit_bytes=VMEM_LIMIT
        ),
        name="gather_grads",
    )(og, w, gate, up, ph, pg, pu, po, ni, pi, member)


def score_kernel(
    n, stores, groups, tile,
    parts, store_rows, out,
    feats_in, queries, store_buf, sent, own, back_in,
    store_sem, fs, fr, qs, qr, bs, br,
):
    d = lax.axis_index("mp")
    sx, gx = lax.axis_index("store"), lax.axis_index("group")
    me = sx * groups + gx
    replicas = stores * groups
    examples = parts.shape[1]
    block = own.shape[0]

    load = pltpu.make_async_copy(store_rows, store_buf, store_sem)
    load.start()

    def peer(k):
        return {"mp": lax.rem(d + k, n)}

    def mate(k):
        other = lax.rem(me + k, replicas)
        return {"store": other // groups, "group": lax.rem(other, groups)}

    barrier = pltpu.get_barrier_semaphore()
    for k in range(1, n):
        pl.semaphore_signal(barrier, inc=1, device_id=peer(k), device_id_type=MESH)
    for k in range(1, replicas):
        pl.semaphore_signal(barrier, inc=1, device_id=mate(k), device_id_type=MESH)
    pl.semaphore_wait(barrier, n + replicas - 2)

    def feats_copy(k):
        return pltpu.make_async_remote_copy(
            src_ref=parts.at[lax.rem(d + k, n)], dst_ref=feats_in.at[k - 1],
            send_sem=fs.at[k - 1], recv_sem=fr.at[k - 1],
            device_id=peer(k), device_id_type=MESH,
        )

    for k in range(1, n):
        feats_copy(k).start()
    total = parts[d]
    for k in range(1, n):
        feats_copy(k).wait_recv()
        total += feats_in[k - 1]
    my_rows = pl.ds(pl.multiple_of(me * examples, examples), examples)
    queries[my_rows, :] = total.astype(jnp.bfloat16)

    def query_copy(k):
        return pltpu.make_async_remote_copy(
            src_ref=queries.at[my_rows, :], dst_ref=queries.at[my_rows, :],
            send_sem=qs.at[k - 1], recv_sem=qr.at[k - 1],
            device_id=mate(k), device_id_type=MESH,
        )

    for k in range(1, replicas):
        query_copy(k).start()
    load.wait()
    for k in range(1, replicas):
        query_copy(k).wait_recv()

    def scores(j, carry):
        cols = pl.ds(pl.multiple_of(j * tile, tile), tile)
        part = lax.dot_general(
            queries[...], store_buf[cols, :], NT, preferred_element_type=jnp.float32
        )
        for p in range(n):
            piece = part[p * block:(p + 1) * block, :]
            sent[p, :, cols] = piece.astype(sent.dtype)

            @pl.when(p == d)
            def _():
                own[:, cols] = piece

        return carry

    lax.fori_loop(0, store_buf.shape[0] // tile, scores, 0)

    def back_copy(k):
        return pltpu.make_async_remote_copy(
            src_ref=sent.at[lax.rem(d + k, n)], dst_ref=back_in.at[k - 1],
            send_sem=bs.at[k - 1], recv_sem=br.at[k - 1],
            device_id=peer(k), device_id_type=MESH,
        )

    for k in range(1, n):
        back_copy(k).start()
    for k in range(1, n):
        back_copy(k).wait_recv()
        own[...] += back_in[k - 1].astype(jnp.float32)
    out[...] = own[...]
    for k in range(1, n):
        feats_copy(k).wait_send()
        back_copy(k).wait_send()
    for k in range(1, replicas):
        query_copy(k).wait_send()


def scored(n, stores, groups, parts, datastore):
    _, examples, width = parts.shape
    count = datastore.shape[0]
    replicas = stores * groups
    block = replicas * examples // n
    sent = jnp.bfloat16 if block % 16 == 0 else jnp.float32
    vmem = pl.BlockSpec(memory_space=pltpu.VMEM)
    dma = pltpu.SemaphoreType.DMA
    return pl.pallas_call(
        functools.partial(score_kernel, n, stores, groups, tile_of(count, 512)),
        out_shape=jax.ShapeDtypeStruct((block, count), jnp.float32),
        in_specs=[vmem, pl.BlockSpec(memory_space=pl.ANY)],
        out_specs=vmem,
        scratch_shapes=[
            pltpu.VMEM((n - 1, examples, width), jnp.float32),
            pltpu.VMEM((replicas * examples, width), jnp.bfloat16),
            pltpu.VMEM(datastore.shape, jnp.bfloat16),
            pltpu.VMEM((n, block, count), sent),
            pltpu.VMEM((block, count), jnp.float32),
            pltpu.VMEM((n - 1, block, count), sent),
            dma(()), dma((n - 1,)), dma((n - 1,)),
            dma((replicas - 1,)), dma((replicas - 1,)),
            dma((n - 1,)), dma((n - 1,)),
        ],
        compiler_params=pltpu.CompilerParams(
            collective_id=1, has_side_effects=True, vmem_limit_bytes=VMEM_LIMIT
        ),
        name="exchange_scores",
    )(parts, datastore)


def on_device(
    n, stores, groups,
    gate_pre, up_pre, out_grad, normed_in, lengths, w_down,
    proj_hidden, proj_gate, proj_up, proj_outgrad, proj_input, datastore,
):
    count = gate_pre.shape[1]
    r = proj_hidden.shape[1]
    example_lengths = lengths[0]
    examples = example_lengths.shape[0]
    order = jnp.arange(examples, dtype=jnp.int32)
    ends = jnp.sum(
        jnp.where(order[None, :] <= order[:, None], example_lengths[None, :], 0), axis=1
    )
    starts = ends - example_lengths
    positions = jnp.arange(count, dtype=jnp.int32)
    member = (
        (positions[None, :] >= starts[:, None]) & (positions[None, :] < ends[:, None])
    ).astype(jnp.float32)

    down, both = gathered(
        n, out_grad[0], w_down, gate_pre[0], up_pre[0],
        proj_hidden.T, proj_gate.T, proj_up.T, proj_outgrad.T, normed_in[0],
        proj_input.T, member.reshape(examples, n, -1).transpose(1, 0, 2),
    )
    down = down.reshape(examples, r, r)
    both = both.reshape(examples, r, 2 * r)
    feats = jnp.concatenate([down, both[:, :, :r], both[:, :, r:]], axis=1)
    parts = feats.reshape(examples, n, -1).transpose(1, 0, 2)
    return scored(n, stores, groups, parts, datastore)


def solution(mesh):
    sizes = mesh.shape
    return jax.shard_map(
        functools.partial(on_device, sizes["mp"], sizes["store"], sizes["group"]),
        mesh=mesh,
        in_specs=(
            P(("store", "group"), None, "mp"),
            P(("store", "group"), None, "mp"),
            P(("store", "group"), "mp", None),
            P(("store", "group"), "mp", None),
            P(("store", "group"), None),
            P("mp", None),
            P("mp", None),
            P("mp", None),
            P("mp", None),
            P(),
            P(),
            P(("store", "group"), "mp"),
        ),
        out_specs=P("mp", ("store", "group")),
        check_vma=False,
    )
```
